128 devices in a mesh: ctx: 8 (over x, y_lo), ch: 16 (over z, y_hi, core).
Axes of the slice: x: 4, y: 4 (y_hi: 2, y_lo: 2; y = y_hi * 2 + y_lo), z: 4, core: 2. Of those that a mesh axis runs over, the one named last changes fastest.
Arguments:
- tokens: bfloat16 [4096, 8192], P('ctx', 'ch'), may hold values from -6 to 6
- proj_value: bfloat16 [8192, 8192], P(None, 'ch'), may hold values from -0.0625 to 0.0625
- proj_gate: bfloat16 [8192, 8192], P(None, 'ch'), may hold values from -0.0625 to 0.0625
- conv_filter: bfloat16 [8192, 4096], P('ch', 'ctx'), may hold values from -4 to 4
- proj_output: bfloat16 [8192, 8192], P('ch'), may hold values from -0.0625 to 0.0625
Outputs:
- mixed: bfloat16 [4096, 8192], P('ctx', 'ch')
The draws below stay inside these ranges and needn't reach their ends.
All inputs are finite; a program needn't handle non-finite values.
Results may differ from the reference program's by a relative error of at most 0.024.
Values may be sent and summed in bfloat16 or wider, within the bound.
A program may use at most 128 MiB of HBM per device.

```python
import math
import jax
import jax.numpy as jnp
from jax import lax

D = 8192
C = 8192
TOKENS = 4096
BLOCK = 512


def draw_conv_filter(key, part):
    key = jax.random.fold_in(key, 7)
    rate_key, noise_key = jax.random.split(key)
    length = TOKENS
    lograte = jax.random.uniform(rate_key, (C, 1), jnp.float32, math.log(0.5 / length), math.log(1.0 / 30.0))
    noise = jax.random.normal(noise_key, (C, length), jnp.float32)
    rate = jnp.exp(lograte)
    places = jnp.arange(length, dtype=jnp.float32)[None, :]
    scaling = jnp.sqrt((1.0 - jnp.exp(-2.0 * rate)) / (1.0 - jnp.exp(-2.0 * rate * length)))
    return (noise * jnp.exp(-rate * places) * scaling).astype(jnp.bfloat16)


def shard_levels(rng, extent, cuts, smallest, largest):
    gain = 1.0
    for axis_at, shards_of in cuts:
        heights = jax.random.uniform(jax.random.fold_in(jax.random.fold_in(rng, 6), axis_at), (shards_of,), jnp.float32, smallest / len(cuts), largest / len(cuts))
        gain = gain * jnp.repeat(jnp.exp(heights), extent[axis_at] // shards_of).reshape((-1,) + (1,) * (len(extent) - 1 - axis_at))
    return gain


def normal_values(stream_key, dims, width, limit, shards=(), kind=jnp.bfloat16):
    array = jax.random.normal(stream_key, dims, jnp.float32) * width
    if len(shards) > 0:
        array = shard_levels(stream_key, dims, shards, -0.22, 0.18) * array
    return jnp.clip(array, min=-limit, max=limit).astype(kind)


def setup_inputs(seed: int = 0) -> dict:
    seeds = jax.random.split(jax.random.key(seed), 6)
    tokens = normal_values(seeds[0], (TOKENS, D), 1.0, 6.0, ((0, 8), (1, 16)))
    proj_value = normal_values(seeds[1], (D, C), D ** -0.5, 0.0625, ((1, 16),))
    proj_gate = normal_values(seeds[2], (D, C), D ** -0.5, 0.0625, ((1, 16),))
    conv_filter = draw_conv_filter(jax.random.fold_in(seeds[5], 71), 0)
    proj_output = normal_values(seeds[4], (C, D), C ** -0.5, 0.0625, ((0, 16),))
    return {"tokens": tokens, "proj_value": proj_value, "proj_gate": proj_gate, "conv_filter": conv_filter, "proj_output": proj_output}


def reference(tokens, proj_value, proj_gate, conv_filter, proj_output):
    value = jnp.dot(tokens, proj_value, preferred_element_type=jnp.float32).astype(jnp.bfloat16)
    gate = jnp.dot(tokens, proj_gate, preferred_element_type=jnp.float32).astype(jnp.bfloat16)
    length = tokens.shape[0]
    spectrum = jnp.fft.rfft(value.astype(jnp.float32), n=2 * length, axis=0)
    response = jnp.fft.rfft(conv_filter.astype(jnp.float32), n=2 * length, axis=1)
    conv = jnp.fft.irfft(spectrum * response.T, n=2 * length, axis=0)[:length]
    gated = (conv * gate.astype(jnp.float32)).astype(jnp.bfloat16)

    def accumulate(total, index):
        offset = (index * BLOCK).astype(jnp.int32)
        gated_part = lax.dynamic_slice_in_dim(gated, offset, BLOCK, 1)
        weight_part = lax.dynamic_slice_in_dim(proj_output, offset, BLOCK, 0)
        term = jnp.dot(gated_part, weight_part, preferred_element_type=jnp.float32).astype(jnp.bfloat16)
        term = lax.optimization_barrier(term)
        return total + term.astype(jnp.float32), None

    start_total = jnp.zeros((length, proj_output.shape[1]), jnp.float32)
    total, unused = lax.scan(accumulate, start_total, jnp.arange(C // BLOCK, dtype=jnp.int32))
    return total.astype(jnp.bfloat16)
```

```python
import math

import jax
import jax.numpy as jnp
import numpy as np
from jax import lax
from jax.experimental import pallas as pl
from jax.experimental.pallas import tpu as pltpu
from jax.sharding import PartitionSpec as P

MESH = pl.DeviceIdType.MESH
BF16 = jnp.bfloat16
F32 = jnp.float32
N = 512
CTX = 8
CHIPS = 8
HALF = 256
A0, A1, A, B0, B1, B, ALL = (
    (0, 112),
    (112, 112),
    (0, 224),
    (224, 144),
    (368, 144),
    (224, 288),
    (0, 512),
)
TRANSFERS = 128


def tables():
    k = np.arange(HALF)[:, None]
    n = np.arange(2 * HALF)[None, :]
    angle = math.pi / (2 * HALF) * ((2 * k + 1) * n % (4 * HALF))
    forward = np.concatenate([np.cos(angle), -np.sin(angle)], axis=0)
    inverse = forward[:, HALF:].T * (1.0 / HALF)
    return forward.astype(jnp.bfloat16), inverse.astype(jnp.bfloat16)


def dot(a, b):
    return jnp.dot(a, b, preferred_element_type=F32)


def rows_of(part):
    return pl.ds(part[0], part[1])


def swap(x):
    return pltpu.roll(x, 64, axis=1)


def low_lanes(rows):
    return lax.broadcasted_iota(jnp.int32, (rows, 128), 1) < 64


def kernel(
    tok_hbm, wv_hbm, wg_hbm, filt_hbm, wo_hbm, fwd_hbm, inv_hbm, out_ref,
    G, WV, WG, WO, FWD, INV, TF, acc_v, acc_g, VS, HSND, XR, HR, YS, YR,
    XQ, HQ, XS, HS, YP, GA, GB, RYA, RYB, RP, RM, ss, rs, ls,
):
    ctx = lax.axis_index("ctx")
    ch = lax.axis_index("ch")
    z, yh, c = ch // 4, lax.rem(ch // 2, 2), lax.rem(ch, 2)
    other = 1 - c

    def chip(dz, dy):
        return lax.rem(z + dz + 4, 4) * 2 + (yh if dy == 0 else 1 - yh)

    up = (ctx, chip(1, 0) * 2 + c)
    down = (ctx, chip(-1, 0) * 2 + c)
    over = (ctx, chip(0, 1) * 2 + c)
    sib = (ctx, chip(0, 0) * 2 + other)

    def ring(k):
        return lax.rem(ctx + k, CTX)

    index = {}
    started = {}

    def slot(name):
        if name not in index:
            index[name] = len(index)
        return index[name]

    def send(name, src, dst, to):
        i = slot(name)
        cp = pltpu.make_async_remote_copy(
            src_ref=src, dst_ref=dst, send_sem=ss.at[i], recv_sem=rs.at[i],
            device_id=to, device_id_type=MESH,
        )
        cp.start()
        started[name] = cp

    def arrived(name, region):
        i = slot(name)
        pltpu.make_async_remote_copy(
            src_ref=region, dst_ref=region, send_sem=ss.at[i], recv_sem=rs.at[i],
            device_id=sib, device_id_type=MESH,
        ).wait_recv()

    def drain(prefix):
        for name in [n for n in started if n.startswith(prefix)]:
            started.pop(name).wait_send()

    local = []

    def fetch(src, dst):
        cp = pltpu.make_async_copy(src, dst, ls.at[len(local)])
        local.append(cp)
        cp.start()
        return cp

    barrier = pltpu.get_barrier_semaphore()
    partners = [up, down, over, sib] + [(ring(k), ch) for k in range(1, CTX)]
    for p in partners:
        pl.semaphore_signal(barrier, inc=1, device_id=p, device_id_type=MESH)
    mine = chip(0, 0)
    tok_in = fetch(tok_hbm, G.at[mine * 2 + c])
    filt_in = fetch(filt_hbm, TF)
    order = [(0, 0), (1, 0), (-1, 0), (0, 1), (2, 0), (1, 1), (-1, 1), (2, 1)]
    w_in = {}
    for d in order:
        r = pl.ds(pl.multiple_of(chip(*d) * 1024, 1024), 1024)
        w_in[d] = (fetch(wv_hbm.at[r], WV.at[r]), fetch(wg_hbm.at[r], WG.at[r]))
    fwd_in = fetch(fwd_hbm, FWD)
    inv_in = fetch(inv_hbm, INV)
    tok_in.wait()
    pl.semaphore_wait(barrier, len(partners))

    def piece(d, part, core=None):
        return G.at[chip(*d) * 2 + (c if core is None else core), rows_of(part)]

    def gsend(name, d, part, to):
        send("g_" + name, piece(d, part), piece(d, part), to)

    def gwait(name, d, part):
        arrived("g_" + name, piece(d, part))

    sibs = {}

    def to_sib(d, *parts):
        for part in parts:
            n = len(sibs)
            sibs[n] = (d, part)
            gsend("s%d" % n, d, part, sib)

    def from_sib(d):
        for n in [n for n in sibs if sibs[n][0] == d]:
            arrived("g_s%d" % n, piece(d, sibs.pop(n)[1], other))
            sibs[n] = (None, None)

    gsend("pa", (0, 0), A, up)
    gsend("ma", (0, 0), A, down)
    gsend("y1", (0, 0), B, over)
    gsend("pb", (0, 0), B, up)
    gsend("mb", (0, 0), B, down)
    gsend("y2", (0, 0), A, over)
    to_sib((0, 0), ALL)

    def pack_into(dst, p, top, bot):
        lo = low_lanes(HALF)
        dst[2 * p] = jnp.where(lo, top, swap(bot)).astype(BF16)
        dst[2 * p + 1] = jnp.where(lo, swap(top), bot).astype(BF16)

    filt_in.wait()

    def filt_pack(p, carry):
        block = TF[pl.ds(pl.multiple_of(p * 128, 128), 128), :].astype(F32).T
        pack_into(HSND, p, block[:HALF], block[HALF:])
        return carry

    lax.fori_loop(0, 4, filt_pack, 0)
    for k in (4, 3, 5, 2, 6, 1, 7):
        send("h_%d" % k, HSND.at[ring(k)], HR.at[ctx], (ring(k), ch))
    HR[ctx] = HSND[ctx]

    def project(acc, w, d, first=False):
        q = chip(*d)

        def body(n, carry):
            cols = pl.ds(pl.multiple_of(n * 256, 256), 256)
            r0 = pl.ds(pl.multiple_of(q * 1024, 1024), 512)
            r1 = pl.ds(pl.multiple_of(q * 1024 + 512, 512), 512)
            total = dot(G[2 * q], w[r0, cols]) + dot(G[2 * q + 1], w[r1, cols])
            acc[:, cols] = total if first else acc[:, cols] + total
            return carry

        lax.fori_loop(0, 2, body, 0)

    def both(d, first=False):
        from_sib(d)
        w_in[d][0].wait()
        w_in[d][1].wait()
        project(acc_v, WV, d, first)
        project(acc_g, WG, d, first)

    both((0, 0), True)
    gwait("pa", (-1, 0), A)
    gsend("p5", (-1, 0), A0, up)
    gsend("y3", (-1, 0), A, over)
    gwait("ma", (1, 0), A)
    gsend("m5", (1, 0), A1, down)
    gsend("y4", (1, 0), A, over)
    to_sib((-1, 0), A)
    to_sib((1, 0), A)
    gwait("y1", (0, 1), B)
    gsend("p7", (0, 1), B0, up)
    gsend("m7", (0, 1), B1, down)
    gsend("p8", (0, 1), B1, up)
    gsend("m8", (0, 1), B0, down)
    to_sib((0, 1), B)
    gwait("pb", (-1, 0), B)
    gsend("p6", (-1, 0), B0, up)
    gwait("mb", (1, 0), B)
    gsend("m6", (1, 0), B1, down)
    to_sib((-1, 0), B)
    to_sib((1, 0), B)
    gwait("y2", (0, 1), A)
    to_sib((0, 1), A)
    both((1, 0))
    gwait("p5", (2, 0), A0)
    gsend("y5", (2, 0), A0, over)
    gwait("m5", (2, 0), A1)
    gsend("y6", (2, 0), A1, over)
    to_sib((2, 0), A0, A1)
    both((-1, 0))
    gwait("p7", (-1, 1), B0)
    gsend("p9", (-1, 1), B0, up)
    gwait("m7", (1, 1), B1)
    gsend("m9", (1, 1), B1, down)
    to_sib((-1, 1), B0)
    to_sib((1, 1), B1)

    def out_cols(q, core):
        return pl.ds(pl.multiple_of((2 * q + core) * N, N), N)

    wo_in = []
    for q in range(CHIPS):
        wo_in.append(fetch(wo_hbm.at[:, out_cols(q, c)], WO.at[q, pl.ds(0, N)]))
        send("w_%d" % q, wo_hbm.at[:, out_cols(q, other)], WO.at[q, pl.ds(N, N)], sib)

    both((0, 1))
    gwait("y3", (-1, 1), A)
    to_sib((-1, 1), A)
    gwait("p8", (-1, 1), B1)
    gwait("m8", (1, 1), B0)
    to_sib((-1, 1), B1)
    to_sib((1, 1), B0)
    gwait("p6", (2, 0), B0)
    gwait("m6", (2, 0), B1)
    to_sib((2, 0), B0, B1)
    gwait("y4", (1, 1), A)
    to_sib((1, 1), A)
    both((2, 0))
    both((-1, 1))
    both((1, 1))
    last = (2, 1)
    gwait("y5", last, A0)
    to_sib(last, A0)
    gwait("y6", last, A1)
    to_sib(last, A1)
    gwait("p9", last, B0)
    to_sib(last, B0)
    gwait("m9", last, B1)
    to_sib(last, B1)
    from_sib(last)
    w_in[last][0].wait()
    w_in[last][1].wait()
    project(acc_v, WV, last)

    for p in range(4):
        cols = slice(128 * p, 128 * p + 128)
        pack_into(VS, p, acc_v[:HALF, cols], acc_v[HALF:, cols])
    for k in (4, 3, 5, 2, 6, 1, 7):
        send("v_%d" % k, VS.at[ring(k)], XR.at[ctx], (ring(k), ch))
    XR[ctx] = VS[ctx]
    project(acc_g, WG, last)

    fwd_in.wait()
    inv_in.wait()
    for k in range(1, CTX):
        arrived("h_%d" % k, HR.at[ring(CTX - k)])

    def spread_filter(i, carry):
        lo = low_lanes(HALF)
        h = HR[i].astype(F32)
        s = swap(h)
        HQ[pl.ds(pl.multiple_of(i * N, N), HALF), :] = jnp.where(lo, h, s).astype(BF16)
        HQ[pl.ds(pl.multiple_of(i * N + HALF, HALF), HALF), :] = jnp.where(lo, s, h).astype(BF16)
        return carry

    lax.fori_loop(0, CTX, spread_filter, 0)

    def filter_spectra(j, carry):
        b0 = HQ[pl.ds(pl.multiple_of(j * N, N), HALF), :]
        b1 = HQ[pl.ds(pl.multiple_of(j * N + HALF, HALF), HALF), :]
        s = dot(FWD[:, :HALF], jnp.concatenate([b0, b1], axis=1))
        HS[2 * j] = s[:, :128]
        HS[2 * j + 1] = s[:, 128:]
        return carry

    lax.fori_loop(0, 8, filter_spectra, 0)

    for k in range(1, CTX):
        arrived("v_%d" % k, XR.at[ring(CTX - k)])
    XQ[pl.ds(0, HALF), :] = jnp.zeros((HALF, 128), BF16)
    lo = low_lanes(HALF)
    XQ[pl.ds(HALF, HALF), :] = jnp.where(lo, 0.0, swap(XR[0].astype(F32))).astype(BF16)
    XQ[pl.ds(N, HALF), :] = XR[0]

    def spread_values(i, carry):
        lo = low_lanes(HALF)
        now = XR[i]
        x = jnp.where(lo, now.astype(F32), XR[i - 1].astype(F32))
        XQ[pl.ds(pl.multiple_of(i * N + HALF, HALF), HALF), :] = swap(x).astype(BF16)
        XQ[pl.ds(pl.multiple_of(i * N + N, N), HALF), :] = now
        return carry

    lax.fori_loop(1, CTX, spread_values, 0)

    def value_spectra(j, carry):
        b0 = XQ[pl.ds(pl.multiple_of(j * N, N), N), :]
        b1 = XQ[pl.ds(pl.multiple_of(j * N + HALF, HALF), N), :]
        s = dot(FWD[...], jnp.concatenate([b0, b1], axis=1))
        XS[2 * j] = s[:, :128]
        XS[2 * j + 1] = s[:, 128:]
        return carry

    lax.fori_loop(0, 8, value_spectra, 0)

    def multiply(t, carry):
        re = pl.ds(pl.multiple_of(t * 8, 8), 8)
        im = pl.ds(pl.multiple_of(t * 8 + HALF, 8), 8)
        xr = [XS[s, re, :] for s in range(16)]
        xi = [XS[s, im, :] for s in range(16)]
        yr, yi = [None] * 8, [None] * 8
        for d in range(16):
            hr, hi = HS[d, re, :], HS[d, im, :]
            for i in range(8):
                s = 2 * i - d + 1
                if s < 0:
                    continue
                r = hr * xr[s] - hi * xi[s]
                m = hr * xi[s] + hi * xr[s]
                yr[i] = r if yr[i] is None else yr[i] + r
                yi[i] = m if yi[i] is None else yi[i] + m
        for i in range(8):
            YP[i, re, :] = yr[i]
            YP[i, im, :] = yi[i]
        return carry

    lax.fori_loop(0, HALF // 8, multiply, 0)

    def back(j, carry):
        s = jnp.concatenate([YP[2 * j].astype(BF16), YP[2 * j + 1].astype(BF16)], axis=1)
        y = dot(INV[...], s).astype(BF16)
        YS[2 * j] = y[:, :128]
        YS[2 * j + 1] = y[:, 128:]
        return carry

    lax.fori_loop(0, 4, back, 0)
    for k in (4, 3, 5, 2, 6, 1, 7):
        send("y_%d" % k, YS.at[ring(k)], YR.at[ctx], (ring(k), ch))
    YR[ctx] = YS[ctx]
    drain("g_")
    for k in range(1, CTX):
        arrived("y_%d" % k, YR.at[ring(CTX - k)])

    for p in range(4):
        cols = slice(128 * p, 128 * p + 128)
        r0, r1 = YR[2 * p].astype(F32), YR[2 * p + 1].astype(F32)
        gate = acc_g[:, cols].astype(BF16).astype(F32)
        GA[:HALF, cols] = (jnp.where(lo, r0, swap(r1)) * gate[:HALF]).astype(BF16)
        GA[HALF:, cols] = (jnp.where(lo, swap(r0), r1) * gate[HALF:]).astype(BF16)
    send("a_0", GA, GB, sib)
    for cp in wo_in:
        cp.wait()
    for q in range(CHIPS):
        arrived("w_%d" % q, WO.at[q, pl.ds(N, N)])
    arrived("a_0", GB)

    def mix(*ds):
        for d in ds:
            q = chip(*d)

            def body(n, carry):
                cols = pl.ds(pl.multiple_of(n * 256, 256), 256)
                total = dot(GA[...], WO[q, :N, cols]) + dot(GB[...], WO[q, N:, cols])
                G[q, :, cols] = total.astype(BF16)
                return carry

            lax.fori_loop(0, 2, body, 0)

    def sums(d, part):
        return G.at[chip(*d), rows_of(part)]

    def rsend(name, d, part, buf, to):
        send("r_" + name, sums(d, part), buf, to)

    def radd(name, buf, d, part):
        arrived("r_" + name, buf)
        ref = sums(d, part)
        ref[...] = (ref[...].astype(F32) + buf[...].astype(F32)).astype(BF16)

    nb, n0, n1, na = B[1], A0[1], A1[1], A[1]
    def cut(ref, start, size):
        return ref.at[pl.ds(start, size)]

    off, pos = {}, 0
    for name, size in (
        ("z2y", 144), ("z2o", 144), ("z1y0", 144), ("z1y1", 144), ("z1o0", 144), ("z1o1", 144),
        ("a2", 112), ("a1x", 112), ("a1y", 112),
    ):
        off[name] = (pos, size)
        pos += size

    def rp(name):
        return cut(RP, *off[name])

    def rm(name):
        return cut(RM, *off[name])

    mix((2, 1))
    rsend("ya0", (2, 1), A, RYA.at[0], over)
    rsend("p_z2y", (2, 1), B0, rp("z2y"), up)
    rsend("m_z2y", (2, 1), B1, rm("z2y"), down)
    mix((2, 0))
    rsend("p_z2o", (2, 0), B0, rp("z2o"), up)
    rsend("m_z2o", (2, 0), B1, rm("z2o"), down)
    mix((1, 1), (-1, 1))
    rsend("ya1", (1, 1), A, RYA.at[1], over)
    rsend("ya2", (-1, 1), A, RYA.at[2], over)
    rsend("p_z1y1", (1, 1), B1, rp("z1y1"), up)
    rsend("m_z1y1", (-1, 1), B0, rm("z1y1"), down)
    mix((0, 1))
    rsend("ya3", (0, 1), A, RYA.at[3], over)
    mix((1, 0), (-1, 0))
    rsend("p_z1o1", (1, 0), B1, rp("z1o1"), up)
    rsend("m_z1o1", (-1, 0), B0, rm("z1o1"), down)
    radd("p_z2y", rp("z2y"), (1, 1), B0)
    rsend("p_z1y0", (1, 1), B0, rp("z1y0"), up)
    radd("m_z2y", rm("z2y"), (-1, 1), B1)
    rsend("m_z1y0", (-1, 1), B1, rm("z1y0"), down)
    radd("ya0", RYA.at[0], (2, 0), A)
    rsend("p_a2", (2, 0), A0, rp("a2"), up)
    rsend("m_a2", (2, 0), A1, rm("a2"), down)
    mix((0, 0))
    radd("p_z2o", rp("z2o"), (1, 0), B0)
    rsend("p_z1o0", (1, 0), B0, rp("z1o0"), up)
    radd("m_z2o", rm("z2o"), (-1, 0), B1)
    rsend("m_z1o0", (-1, 0), B1, rm("z1o0"), down)
    radd("p_z1y1", rp("z1y1"), (0, 1), B1)
    radd("m_z1y1", rm("z1y1"), (0, 1), B0)
    radd("ya1", RYA.at[1], (1, 0), A)
    rsend("p_a1x", (1, 0), A1, rp("a1x"), up)
    radd("p_z1y0", rp("z1y0"), (0, 1), B0)
    radd("m_z1y0", rm("z1y0"), (0, 1), B1)
    rsend("yb", (0, 1), B, RYB, over)
    radd("ya2", RYA.at[2], (-1, 0), A)
    rsend("m_a1x", (-1, 0), A0, rm("a1x"), down)
    radd("p_a2", rp("a2"), (1, 0), A0)
    rsend("p_a1y", (1, 0), A0, rp("a1y"), up)
    radd("m_a2", rm("a2"), (-1, 0), A1)
    rsend("m_a1y", (-1, 0), A1, rm("a1y"), down)

    def total(part, *bufs):
        value = sums((0, 0), part)[...].astype(F32)
        for b in bufs:
            value = value + b[...].astype(F32)
        out_ref[rows_of(part), :] = value.astype(BF16)

    arrived("r_ya3", RYA.at[3])
    for name in ("z1o1", "z1o0"):
        arrived("r_p_" + name, rp(name))
        arrived("r_m_" + name, rm(name))
    arrived("r_yb", RYB)
    total(B0, rp("z1o0"), rm("z1o1"), cut(RYB, 0, 144))
    total(B1, rp("z1o1"), rm("z1o0"), cut(RYB, 144, 144))
    for name in ("a1x", "a1y"):
        arrived("r_p_" + name, rp(name))
        arrived("r_m_" + name, rm(name))
    total(A0, cut(RYA.at[3], 0, 112), rp("a1y"), rm("a1x"))
    total(A1, cut(RYA.at[3], 112, 112), rp("a1x"), rm("a1y"))
    drain("")


def on_device(tokens, proj_value, proj_gate, conv_filter, proj_output):
    forward, inverse = tables()
    anywhere = pl.BlockSpec(memory_space=pl.ANY)
    vm = pltpu.VMEM
    return pl.pallas_call(
        kernel,
        out_shape=jax.ShapeDtypeStruct((N, N), BF16),
        in_specs=[anywhere] * 7,
        out_specs=pl.BlockSpec(memory_space=pltpu.VMEM),
        scratch_shapes=[
            vm((16, N, N), BF16),
            vm((8192, N), BF16),
            vm((8192, N), BF16),
            vm((CHIPS, 2 * N, N), BF16),
            vm((2 * HALF, 2 * HALF), BF16),
            vm((HALF, 2 * HALF), BF16),
            vm((N, N), BF16),
            vm((N, N), F32),
            vm((N, N), F32),
            vm((CTX, HALF, 128), BF16),
            vm((CTX, HALF, 128), BF16),
            vm((CTX, HALF, 128), BF16),
            vm((CTX, HALF, 128), BF16),
            vm((CTX, HALF, 128), BF16),
            vm((CTX, HALF, 128), BF16),
            vm((17 * HALF, 128), BF16),
            vm((16 * HALF, 128), BF16),
            vm((16, N, 128), F32),
            vm((16, N, 128), F32),
            vm((8, N, 128), F32),
            vm((N, N), BF16),
            vm((N, N), BF16),
            vm((4, A[1], N), BF16),
            vm((B[1], N), BF16),
            vm((1200, N), BF16),
            vm((1200, N), BF16),
            pltpu.SemaphoreType.DMA((TRANSFERS,)),
            pltpu.SemaphoreType.DMA((TRANSFERS,)),
            pltpu.SemaphoreType.DMA((40,)),
        ],
        compiler_params=pltpu.CompilerParams(
            collective_id=0, has_side_effects=True, vmem_limit_bytes=60 * 2**20
        ),
        name="hyena_block",
    )(
        tokens, proj_value, proj_gate, conv_filter, proj_output,
        jnp.asarray(forward), jnp.asarray(inverse),
    )


def solution(mesh):
    in_specs = (P("ctx", "ch"), P(None, "ch"), P(None, "ch"), P("ch", "ctx"), P("ch", None))
    return jax.shard_map(
        on_device, mesh=mesh, in_specs=in_specs, out_specs=P("ctx", "ch"), check_vma=False
    )
```

```python
import math

import jax
import jax.numpy as jnp
import numpy as np
from jax import lax
from jax.experimental import pallas as pl
from jax.experimental.pallas import tpu as pltpu
from jax.sharding import PartitionSpec as P

MESH = pl.DeviceIdType.MESH
BF16 = jnp.bfloat16
F32 = jnp.float32
N = 512
CTX = 8
CHIPS = 8
HALF = 256
A0, A1, A, B0, B1, B, ALL = (
    (0, 112),
    (112, 112),
    (0, 224),
    (224, 144),
    (368, 144),
    (224, 288),
    (0, 512),
)
GA0, GA1, GA_, GB0, GB1, GB_ = ((0, 80), (80, 80), (0, 160), (160, 176), (336, 176), (160, 352))
TRANSFERS = 128


def tables():
    k = np.concatenate([np.arange(0, HALF, 2), np.arange(1, HALF, 2)])[:, None]
    n = np.arange(2 * HALF)[None, :]
    angle = math.pi / (2 * HALF) * ((2 * k + 1) * n % (4 * HALF))
    forward = np.concatenate([np.cos(angle), -np.sin(angle)], axis=0)
    inverse = forward[:, HALF:].T * (1.0 / HALF)
    return forward[:, :HALF].astype(jnp.bfloat16), inverse.astype(jnp.bfloat16)


def dot(a, b):
    return jnp.dot(a, b, preferred_element_type=F32)


def rows_of(part):
    return pl.ds(part[0], part[1])


def swap(x):
    return pltpu.roll(x, 64, axis=1)


def low_lanes(rows):
    return lax.broadcasted_iota(jnp.int32, (rows, 128), 1) < 64


def kernel(
    tok_hbm, wv_hbm, wg_hbm, filt_hbm, wo_hbm, fwd_hbm, inv_hbm, out_ref,
    G, WV, WG, WO, FWD, INV, TF, acc_v, acc_g, VS, HSND, XR, HR, YS, YR,
    HQ, XS, HS, YP, GA, GB, RYA, RYB, RP, RM, ss, rs, ls,
):
    ctx = lax.axis_index("ctx")
    ch = lax.axis_index("ch")
    z, yh, c = ch // 4, lax.rem(ch // 2, 2), lax.rem(ch, 2)
    other = 1 - c

    def chip(dz, dy):
        return lax.rem(z + dz + 4, 4) * 2 + (yh if dy == 0 else 1 - yh)

    up = (ctx, chip(1, 0) * 2 + c)
    down = (ctx, chip(-1, 0) * 2 + c)
    over = (ctx, chip(0, 1) * 2 + c)
    sib = (ctx, chip(0, 0) * 2 + other)

    def ring(k):
        return lax.rem(ctx + k, CTX)

    index = {}
    started = {}

    def slot(name):
        if name not in index:
            index[name] = len(index)
        return index[name]

    def send(name, src, dst, to):
        i = slot(name)
        cp = pltpu.make_async_remote_copy(
            src_ref=src, dst_ref=dst, send_sem=ss.at[i], recv_sem=rs.at[i],
            device_id=to, device_id_type=MESH,
        )
        cp.start()
        started[name] = cp

    def arrived(name, region):
        i = slot(name)
        pltpu.make_async_remote_copy(
            src_ref=region, dst_ref=region, send_sem=ss.at[i], recv_sem=rs.at[i],
            device_id=sib, device_id_type=MESH,
        ).wait_recv()

    def drain(prefix):
        for name in [n for n in started if n.startswith(prefix)]:
            started.pop(name).wait_send()

    local = []

    def fetch(src, dst):
        cp = pltpu.make_async_copy(src, dst, ls.at[len(local)])
        local.append(cp)
        cp.start()
        return cp

    barrier = pltpu.get_barrier_semaphore()
    partners = [up, down, over, sib] + [(ring(k), ch) for k in range(1, CTX)]
    for p in partners:
        pl.semaphore_signal(barrier, inc=1, device_id=p, device_id_type=MESH)
    mine = chip(0, 0)
    tok_in = fetch(tok_hbm, G.at[mine * 2 + c])
    filt_in = fetch(filt_hbm, TF)
    order = [(0, 0), (1, 0), (-1, 0), (0, 1), (2, 0), (1, 1), (-1, 1), (2, 1)]
    tok_in.wait()
    pl.semaphore_wait(barrier, len(partners))

    def piece(d, part, core=None):
        return G.at[chip(*d) * 2 + (c if core is None else core), rows_of(part)]

    def gsend(name, d, part, to):
        send("g_" + name, piece(d, part), piece(d, part), to)

    def gwait(name, d, part):
        arrived("g_" + name, piece(d, part))

    sibs = {}

    def to_sib(d, *parts):
        for part in parts:
            n = len(sibs)
            sibs[n] = (d, part)
            gsend("s%d" % n, d, part, sib)

    def from_sib(d):
        for n in [n for n in sibs if sibs[n][0] == d]:
            arrived("g_s%d" % n, piece(d, sibs.pop(n)[1], other))
            sibs[n] = (None, None)

    gsend("pa", (0, 0), GA_, up)
    gsend("ma", (0, 0), GA_, down)
    gsend("y1", (0, 0), GB_, over)
    gsend("pb", (0, 0), GB_, up)
    gsend("mb", (0, 0), GB_, down)
    gsend("y2", (0, 0), GA_, over)
    to_sib((0, 0), ALL)
    w_in = {}
    for d in order:
        r = pl.ds(pl.multiple_of(chip(*d) * 1024, 1024), 1024)
        w_in[d] = (fetch(wv_hbm.at[r], WV.at[r]), fetch(wg_hbm.at[r], WG.at[r]))
    fwd_in = fetch(fwd_hbm, FWD)
    inv_in = fetch(inv_hbm, INV)

    def out_cols(q, core):
        return pl.ds(pl.multiple_of((2 * q + core) * N, N), N)

    wo_in = []
    for q in range(CHIPS):
        send("w_%d" % q, wo_hbm.at[:, out_cols(q, other)], WO.at[q, pl.ds(N, N)], sib)
        wo_in.append(fetch(wo_hbm.at[:, out_cols(q, c)], WO.at[q, pl.ds(0, N)]))

    def pack_into(dst, p, top, bot):
        lo = low_lanes(HALF)
        dst[2 * p] = jnp.where(lo, top, swap(bot)).astype(BF16)
        dst[2 * p + 1] = jnp.where(lo, swap(top), bot).astype(BF16)

    filt_in.wait()

    def filt_pack(p, carry):
        block = TF[pl.ds(pl.multiple_of(p * 128, 128), 128), :].astype(F32).T
        pack_into(HSND, p, block[:HALF], block[HALF:])
        return carry

    lax.fori_loop(0, 4, filt_pack, 0)

    def send_filter(*ks):
        for k in ks:
            send("h_%d" % k, HSND.at[ring(k)], HR.at[ctx], (ring(k), ch))

    send_filter(4, 2, 6)
    HR[ctx] = HSND[ctx]

    def project(acc, w, d, first=False, cores=(0, 1)):
        def body(n, carry):
            cols = pl.ds(pl.multiple_of(n * 256, 256), 256)
            total = None
            for core in cores:
                g = chip(*d) * 2 + core
                r = pl.ds(pl.multiple_of(g * N, N), N)
                term = dot(G[g], w[r, cols])
                total = term if total is None else total + term
            acc[:, cols] = total if first else acc[:, cols] + total
            return carry

        lax.fori_loop(0, 2, body, 0)

    def ready(d):
        from_sib(d)
        w_in[d][0].wait()
        w_in[d][1].wait()

    def both(d, first=False):
        ready(d)
        project(acc_v, WV, d, first)
        project(acc_g, WG, d, first)

    both((0, 0), True)
    gwait("pa", (-1, 0), GA_)
    gsend("p5", (-1, 0), GA0, up)
    gsend("y3", (-1, 0), GA_, over)
    gwait("ma", (1, 0), GA_)
    gsend("m5", (1, 0), GA1, down)
    gsend("y4", (1, 0), GA_, over)
    to_sib((-1, 0), GA_)
    to_sib((1, 0), GA_)
    gwait("y1", (0, 1), GB_)
    gsend("p7", (0, 1), GB0, up)
    gsend("m7", (0, 1), GB1, down)
    to_sib((0, 1), GB_)
    gwait("pb", (-1, 0), GB_)
    gsend("p6", (-1, 0), GB0, up)
    gsend("p8", (0, 1), GB1, up)
    gwait("mb", (1, 0), GB_)
    gsend("m6", (1, 0), GB1, down)
    gsend("m8", (0, 1), GB0, down)
    to_sib((1, 0), GB_)
    to_sib((-1, 0), GB_)
    gwait("y2", (0, 1), GA_)
    to_sib((0, 1), GA_)
    send_filter(3, 5, 1, 7)
    gwait("p5", (2, 0), GA0)
    gsend("y5", (2, 0), GA0, over)
    gwait("m5", (2, 0), GA1)
    gsend("y6", (2, 0), GA1, over)
    to_sib((2, 0), GA0, GA1)
    both((1, 0))
    both((-1, 0))
    gwait("p7", (-1, 1), GB0)
    gsend("p9", (-1, 1), GB0, up)
    gwait("m7", (1, 1), GB1)
    gsend("m9", (1, 1), GB1, down)
    to_sib((-1, 1), GB0)
    to_sib((1, 1), GB1)
    both((0, 1))
    gwait("y3", (-1, 1), GA_)
    to_sib((-1, 1), GA_)
    gwait("p6", (2, 0), GB0)
    gwait("m6", (2, 0), GB1)
    to_sib((2, 0), GB0, GB1)
    both((2, 0))
    gwait("y4", (1, 1), GA_)
    to_sib((1, 1), GA_)
    gwait("p8", (-1, 1), GB1)
    gwait("m8", (1, 1), GB0)
    to_sib((-1, 1), GB1)
    to_sib((1, 1), GB0)
    ready((-1, 1))
    project(acc_v, WV, (-1, 1))
    ready((1, 1))
    project(acc_v, WV, (1, 1))
    last = (2, 1)
    gwait("y5", last, GA0)
    to_sib(last, GA0)
    gwait("y6", last, GA1)
    to_sib(last, GA1)
    project(acc_g, WG, (-1, 1))
    gwait("p9", last, GB0)
    to_sib(last, GB0)
    gwait("m9", last, GB1)
    to_sib(last, GB1)
    w_in[last][0].wait()
    w_in[last][1].wait()
    project(acc_v, WV, last, cores=(c,))
    from_sib(last)
    project(acc_v, WV, last, cores=(other,))

    for p in range(4):
        cols = slice(128 * p, 128 * p + 128)
        pack_into(VS, p, acc_v[:HALF, cols], acc_v[HALF:, cols])
    for k in (4, 3, 5, 2, 6, 1, 7):
        send("v_%d" % k, VS.at[ring(k)], XR.at[ctx], (ring(k), ch))
    XR[ctx] = VS[ctx]
    project(acc_g, WG, (1, 1))
    project(acc_g, WG, last)

    fwd_in.wait()
    inv_in.wait()
    for k in range(1, CTX):
        arrived("h_%d" % k, HR.at[ring(CTX - k)])

    def spread_filter(i, carry):
        lo = low_lanes(HALF)
        h = HR[i].astype(F32)
        s = swap(h)
        HQ[pl.ds(pl.multiple_of(i * N, N), HALF), :] = jnp.where(lo, h, s).astype(BF16)
        HQ[pl.ds(pl.multiple_of(i * N + HALF, HALF), HALF), :] = jnp.where(lo, s, h).astype(BF16)
        return carry

    lax.fori_loop(0, CTX, spread_filter, 0)

    def filter_spectra(j, carry):
        b0 = HQ[pl.ds(pl.multiple_of(j * N, N), HALF), :]
        b1 = HQ[pl.ds(pl.multiple_of(j * N + HALF, HALF), HALF), :]
        s = dot(FWD[...], jnp.concatenate([b0, b1], axis=1))
        HS[2 * j] = s[:, :128]
        HS[2 * j + 1] = s[:, 128:]
        return carry

    lax.fori_loop(0, 8, filter_spectra, 0)

    def value_spectrum(i):
        XS[i] = dot(FWD[...], XR[i])

    value_spectrum(ctx)

    for k in (1, 7, 2, 6, 3, 5, 4):
        i = ring(CTX - k)
        arrived("v_%d" % k, XR.at[i])
        value_spectrum(i)

    lo = low_lanes(HALF)

    def multiply(even):
        def body(t, carry):
            re = pl.ds(pl.multiple_of(t * 8, 8), 8)
            im = pl.ds(pl.multiple_of(t * 8 + HALF, 8), 8)
            lo8 = low_lanes(8)
            xr, xi = [], []
            pr = pi = jnp.zeros((8, 128), F32)
            for i in range(8):
                ur, ui = XS[i, re, :], XS[i, im, :]
                mr = swap(jnp.where(lo8, ur, pr))
                mi = swap(jnp.where(lo8, ui, pi))
                if even:
                    xr += [pr + mi, mr + ui]
                    xi += [pi - mr, mi - ur]
                else:
                    xr += [pr - mi, mr - ui]
                    xi += [pi + mr, mi + ur]
                pr, pi = ur, ui
            yr, yi = [None] * 8, [None] * 8
            for d in range(16):
                hr, hi = HS[d, re, :], HS[d, im, :]
                for i in range(8):
                    s = 2 * i - d + 1
                    if s < 0:
                        continue
                    r = hr * xr[s] - hi * xi[s]
                    m = hr * xi[s] + hi * xr[s]
                    yr[i] = r if yr[i] is None else yr[i] + r
                    yi[i] = m if yi[i] is None else yi[i] + m
            for i in range(8):
                YP[i, re, :] = yr[i]
                YP[i, im, :] = yi[i]
            return carry

        return body

    lax.fori_loop(0, HALF // 16, multiply(True), 0)
    lax.fori_loop(HALF // 16, HALF // 8, multiply(False), 0)

    for k in (4, 3, 5, 2, 6, 1, 7, 0):
        i = ring(k)
        y = dot(INV[...], YP[i].astype(BF16)).astype(BF16)
        if k:
            YS[i] = y
            send("y_%d" % k, YS.at[i], YR.at[ctx], (i, ch))
        else:
            YR[ctx] = y
    drain("g_")
    for k in range(1, CTX):
        arrived("y_%d" % k, YR.at[ring(CTX - k)])

    for p in range(4):
        cols = slice(128 * p, 128 * p + 128)
        r0, r1 = YR[2 * p].astype(F32), YR[2 * p + 1].astype(F32)
        gate = acc_g[:, cols].astype(BF16).astype(F32)
        GA[:HALF, cols] = (jnp.where(lo, r0, swap(r1)) * gate[:HALF]).astype(BF16)
        GA[HALF:, cols] = (jnp.where(lo, swap(r0), r1) * gate[HALF:]).astype(BF16)
        send("a_%d" % p, GA.at[:, cols], GB.at[:, cols], sib)
    for cp in wo_in:
        cp.wait()
    for q in range(CHIPS):
        arrived("w_%d" % q, WO.at[q, pl.ds(N, N)])
    for p in range(4):
        arrived("a_%d" % p, GB.at[:, 128 * p : 128 * p + 128])

    def mix(*ds):
        for d in ds:
            q = chip(*d)

            def body(n, carry):
                cols = pl.ds(pl.multiple_of(n * 256, 256), 256)
                total = dot(GA[...], WO[q, :N, cols]) + dot(GB[...], WO[q, N:, cols])
                G[q, :, cols] = total.astype(BF16)
                return carry

            lax.fori_loop(0, 2, body, 0)

    def sums(d, part):
        return G.at[chip(*d), rows_of(part)]

    def rsend(name, d, part, buf, to):
        send("r_" + name, sums(d, part), buf, to)

    def radd(name, buf, d, part):
        arrived("r_" + name, buf)
        ref = sums(d, part)
        ref[...] = (ref[...].astype(F32) + buf[...].astype(F32)).astype(BF16)

    nb, n0, n1, na = B[1], A0[1], A1[1], A[1]
    def cut(ref, start, size):
        return ref.at[pl.ds(start, size)]

    off, pos = {}, 0
    for name, size in (
        ("z2y", 144), ("z2o", 144), ("z1y0", 144), ("z1y1", 144), ("z1o0", 144), ("z1o1", 144),
        ("a2", 112), ("a1x", 112), ("a1y", 112),
    ):
        off[name] = (pos, size)
        pos += size

    def rp(name):
        return cut(RP, *off[name])

    def rm(name):
        return cut(RM, *off[name])

    mix((2, 1))
    rsend("ya0", (2, 1), A, RYA.at[0], over)
    rsend("p_z2y", (2, 1), B0, rp("z2y"), up)
    rsend("m_z2y", (2, 1), B1, rm("z2y"), down)
    mix((2, 0))
    rsend("p_z2o", (2, 0), B0, rp("z2o"), up)
    rsend("m_z2o", (2, 0), B1, rm("z2o"), down)
    mix((1, 1), (-1, 1))
    rsend("ya1", (1, 1), A, RYA.at[1], over)
    rsend("ya2", (-1, 1), A, RYA.at[2], over)
    rsend("p_z1y1", (1, 1), B1, rp("z1y1"), up)
    rsend("m_z1y1", (-1, 1), B0, rm("z1y1"), down)
    mix((0, 1))
    rsend("ya3", (0, 1), A, RYA.at[3], over)
    mix((1, 0), (-1, 0))
    rsend("p_z1o1", (1, 0), B1, rp("z1o1"), up)
    rsend("m_z1o1", (-1, 0), B0, rm("z1o1"), down)
    radd("p_z2y", rp("z2y"), (1, 1), B0)
    rsend("p_z1y0", (1, 1), B0, rp("z1y0"), up)
    radd("m_z2y", rm("z2y"), (-1, 1), B1)
    rsend("m_z1y0", (-1, 1), B1, rm("z1y0"), down)
    radd("ya0", RYA.at[0], (2, 0), A)
    rsend("p_a2", (2, 0), A0, rp("a2"), up)
    rsend("m_a2", (2, 0), A1, rm("a2"), down)
    mix((0, 0))
    radd("p_z2o", rp("z2o"), (1, 0), B0)
    rsend("p_z1o0", (1, 0), B0, rp("z1o0"), up)
    radd("m_z2o", rm("z2o"), (-1, 0), B1)
    rsend("m_z1o0", (-1, 0), B1, rm("z1o0"), down)
    radd("p_z1y1", rp("z1y1"), (0, 1), B1)
    radd("m_z1y1", rm("z1y1"), (0, 1), B0)
    radd("ya1", RYA.at[1], (1, 0), A)
    rsend("p_a1x", (1, 0), A1, rp("a1x"), up)
    radd("p_z1y0", rp("z1y0"), (0, 1), B0)
    radd("m_z1y0", rm("z1y0"), (0, 1), B1)
    rsend("yb", (0, 1), B, RYB, over)
    radd("ya2", RYA.at[2], (-1, 0), A)
    rsend("m_a1x", (-1, 0), A0, rm("a1x"), down)
    radd("p_a2", rp("a2"), (1, 0), A0)
    rsend("p_a1y", (1, 0), A0, rp("a1y"), up)
    radd("m_a2", rm("a2"), (-1, 0), A1)
    rsend("m_a1y", (-1, 0), A1, rm("a1y"), down)

    def total(part, *bufs):
        value = sums((0, 0), part)[...].astype(F32)
        for b in bufs:
            value = value + b[...].astype(F32)
        out_ref[rows_of(part), :] = value.astype(BF16)

    arrived("r_ya3", RYA.at[3])
    for name in ("z1o1", "z1o0"):
        arrived("r_p_" + name, rp(name))
        arrived("r_m_" + name, rm(name))
    arrived("r_yb", RYB)
    total(B0, rp("z1o0"), rm("z1o1"), cut(RYB, 0, 144))
    total(B1, rp("z1o1"), rm("z1o0"), cut(RYB, 144, 144))
    for name in ("a1x", "a1y"):
        arrived("r_p_" + name, rp(name))
        arrived("r_m_" + name, rm(name))
    total(A0, cut(RYA.at[3], 0, 112), rp("a1y"), rm("a1x"))
    total(A1, cut(RYA.at[3], 112, 112), rp("a1x"), rm("a1y"))
    drain("")


def on_device(tokens, proj_value, proj_gate, conv_filter, proj_output):
    forward, inverse = tables()
    anywhere = pl.BlockSpec(memory_space=pl.ANY)
    vm = pltpu.VMEM
    return pl.pallas_call(
        kernel,
        out_shape=pltpu.VMEM((N, N), BF16),
        in_specs=[anywhere] * 7,
        out_specs=pl.BlockSpec(memory_space=pltpu.VMEM),
        scratch_shapes=[
            vm((16, N, N), BF16),
            vm((8192, N), BF16),
            vm((8192, N), BF16),
            vm((CHIPS, 2 * N, N), BF16),
            vm((2 * HALF, HALF), BF16),
            vm((HALF, 2 * HALF), BF16),
            vm((N, N), BF16),
            vm((N, N), F32),
            vm((N, N), F32),
            vm((CTX, HALF, 128), BF16),
            vm((CTX, HALF, 128), BF16),
            vm((CTX, HALF, 128), BF16),
            vm((CTX, HALF, 128), BF16),
            vm((CTX, HALF, 128), BF16),
            vm((CTX, HALF, 128), BF16),
            vm((16 * HALF, 128), BF16),
            vm((8, N, 128), F32),
            vm((16, N, 128), F32),
            vm((8, N, 128), F32),
            vm((N, N), BF16),
            vm((N, N), BF16),
            vm((4, A[1], N), BF16),
            vm((B[1], N), BF16),
            vm((1200, N), BF16),
            vm((1200, N), BF16),
            pltpu.SemaphoreType.DMA((TRANSFERS,)),
            pltpu.SemaphoreType.DMA((TRANSFERS,)),
            pltpu.SemaphoreType.DMA((40,)),
        ],
        compiler_params=pltpu.CompilerParams(
            collective_id=0, has_side_effects=True, vmem_limit_bytes=56 * 2**20
        ),
        name="hyena_block",
    )(
        tokens, proj_value, proj_gate, conv_filter, proj_output,
        jnp.asarray(forward), jnp.asarray(inverse),
    )


def solution(mesh):
    in_specs = (P("ctx", "ch"), P(None, "ch"), P(None, "ch"), P("ch", "ctx"), P("ch", None))
    return jax.shard_map(
        on_device, mesh=mesh, in_specs=in_specs, out_specs=P("ctx", "ch"), check_vma=False
    )
```

```python
import math

import jax
import jax.numpy as jnp
import numpy as np
from jax import lax
from jax.experimental import pallas as pl
from jax.experimental.pallas import tpu as pltpu
from jax.sharding import PartitionSpec as P

MESH = pl.DeviceIdType.MESH
BF16 = jnp.bfloat16
F32 = jnp.float32
N = 512
CTX = 8
CHIPS = 8
HALF = 256
ALL = (0, 512)
QUARTER = 128


def parts(base, *sizes):
    a0, a1, b0, b1 = sizes
    return (
        (base, a0), (base + a0, a1), (base, a0 + a1),
        (base + a0 + a1, b0), (base + a0 + a1 + b0, b1), (base + a0 + a1, b0 + b1),
    )


WAVES = (parts(0, 48, 48, 80, 80), parts(256, 48, 64, 80, 64))
GA0, GA1, GA_, GB0, GB1, GB_ = ((0, 80), (80, 80), (0, 160), (160, 176), (336, 176), (160, 352))
TRANSFERS = 192


def tables():
    k = np.concatenate([np.arange(0, HALF, 2), np.arange(1, HALF, 2)])[:, None]
    n = np.arange(2 * HALF)[None, :]
    angle = math.pi / (2 * HALF) * ((2 * k + 1) * n % (4 * HALF))
    forward = np.concatenate([np.cos(angle), -np.sin(angle)], axis=0)
    inverse = forward[:, HALF:].T * (1.0 / HALF)
    return forward[:, :HALF].astype(jnp.bfloat16), inverse.astype(jnp.bfloat16)


def dot(a, b):
    return jnp.dot(a, b, preferred_element_type=F32)


def rows_of(part):
    return pl.ds(part[0], part[1])


def swap(x):
    return pltpu.roll(x, 64, axis=1)


def low_lanes(rows):
    return lax.broadcasted_iota(jnp.int32, (rows, 128), 1) < 64


def kernel(
    tok_hbm, wv_hbm, wg_hbm, filt_hbm, wo_hbm, fwd_hbm, inv_hbm, out_ref,
    G, WV, WG, WO, FWD, INV, TF, acc_v, acc_g, VS, HSND, XR, HR, YS, YR,
    HQ, XS, HS, YP, GA, GB, RYA, RYB, RP, RM, ss, rs, ls,
):
    ctx = lax.axis_index("ctx")
    ch = lax.axis_index("ch")
    z, yh, c = ch // 4, lax.rem(ch // 2, 2), lax.rem(ch, 2)
    other = 1 - c

    def chip(dz, dy):
        return lax.rem(z + dz + 4, 4) * 2 + (yh if dy == 0 else 1 - yh)

    up = (ctx, chip(1, 0) * 2 + c)
    down = (ctx, chip(-1, 0) * 2 + c)
    over = (ctx, chip(0, 1) * 2 + c)
    sib = (ctx, chip(0, 0) * 2 + other)

    def ring(k):
        return lax.rem(ctx + k, CTX)

    index = {}
    started = {}

    def slot(name):
        if name not in index:
            index[name] = len(index)
        return index[name]

    def send(name, src, dst, to):
        i = slot(name)
        cp = pltpu.make_async_remote_copy(
            src_ref=src, dst_ref=dst, send_sem=ss.at[i], recv_sem=rs.at[i],
            device_id=to, device_id_type=MESH,
        )
        cp.start()
        started[name] = cp

    def arrived(name, region):
        i = slot(name)
        pltpu.make_async_remote_copy(
            src_ref=region, dst_ref=region, send_sem=ss.at[i], recv_sem=rs.at[i],
            device_id=sib, device_id_type=MESH,
        ).wait_recv()

    def drain(prefix):
        for name in [n for n in started if n.startswith(prefix)]:
            started.pop(name).wait_send()

    local = []

    def fetch(src, dst):
        cp = pltpu.make_async_copy(src, dst, ls.at[len(local)])
        local.append(cp)
        cp.start()
        return cp

    barrier = pltpu.get_barrier_semaphore()
    partners = [up, down, over, sib] + [(ring(k), ch) for k in range(1, CTX)]
    for p in partners:
        pl.semaphore_signal(barrier, inc=1, device_id=p, device_id_type=MESH)
    mine = chip(0, 0)
    tok_in = fetch(tok_hbm, G.at[mine * 2 + c])
    filt_in = fetch(filt_hbm, TF)
    order = [(0, 0), (1, 0), (-1, 0), (0, 1), (2, 0), (1, 1), (-1, 1), (2, 1)]
    tok_in.wait()
    pl.semaphore_wait(barrier, len(partners))

    def piece(d, part, core=None):
        return G.at[chip(*d) * 2 + (c if core is None else core), rows_of(part)]

    def gsend(name, d, part, to):
        send("g_" + name, piece(d, part), piece(d, part), to)

    def gwait(name, d, part):
        arrived("g_" + name, piece(d, part))

    sibs = {}

    def to_sib(d, *parts):
        for part in parts:
            n = len(sibs)
            sibs[n] = (d, part)
            gsend("s%d" % n, d, part, sib)

    def from_sib(d):
        for n in [n for n in sibs if sibs[n][0] == d]:
            arrived("g_s%d" % n, piece(d, sibs.pop(n)[1], other))
            sibs[n] = (None, None)

    gsend("pa", (0, 0), GA_, up)
    gsend("ma", (0, 0), GA_, down)
    gsend("y1", (0, 0), GB_, over)
    gsend("pb", (0, 0), GB_, up)
    gsend("mb", (0, 0), GB_, down)
    gsend("y2", (0, 0), GA_, over)
    to_sib((0, 0), ALL)
    w_in = {}
    for d in order:
        r = pl.ds(pl.multiple_of(chip(*d) * 1024, 1024), 1024)
        w_in[d] = (fetch(wv_hbm.at[r], WV.at[r]), fetch(wg_hbm.at[r], WG.at[r]))
    fwd_in = fetch(fwd_hbm, FWD)
    inv_in = fetch(inv_hbm, INV)

    def out_cols(q, core):
        return pl.ds(pl.multiple_of((2 * q + core) * N, N), N)

    wo_in = []
    for q in range(CHIPS):
        send("w_%d" % q, wo_hbm.at[:, out_cols(q, other)], WO.at[q, pl.ds(N, N)], sib)
        wo_in.append(fetch(wo_hbm.at[:, out_cols(q, c)], WO.at[q, pl.ds(0, N)]))

    def pack_into(dst, p, top, bot):
        lo = low_lanes(HALF)
        dst[2 * p] = jnp.where(lo, top, swap(bot)).astype(BF16)
        dst[2 * p + 1] = jnp.where(lo, swap(top), bot).astype(BF16)

    filt_in.wait()

    def filt_pack(p, carry):
        block = TF[pl.ds(pl.multiple_of(p * 128, 128), 128), :].astype(F32).T
        pack_into(HSND, p, block[:HALF], block[HALF:])
        return carry

    lax.fori_loop(0, 4, filt_pack, 0)

    def send_filter(*ks):
        for k in ks:
            send("h_%d" % k, HSND.at[ring(k)], HR.at[ctx], (ring(k), ch))

    send_filter(4, 2, 6)
    HR[ctx] = HSND[ctx]

    def project(acc, w, d, first=False, cores=(0, 1)):
        def body(n, carry):
            cols = pl.ds(pl.multiple_of(n * 256, 256), 256)
            total = None
            for core in cores:
                g = chip(*d) * 2 + core
                r = pl.ds(pl.multiple_of(g * N, N), N)
                term = dot(G[g], w[r, cols])
                total = term if total is None else total + term
            acc[:, cols] = total if first else acc[:, cols] + total
            return carry

        lax.fori_loop(0, 2, body, 0)

    def ready(d):
        from_sib(d)
        w_in[d][0].wait()
        w_in[d][1].wait()

    def both(d, first=False):
        ready(d)
        project(acc_v, WV, d, first)
        project(acc_g, WG, d, first)

    both((0, 0), True)
    gwait("pa", (-1, 0), GA_)
    gsend("p5", (-1, 0), GA0, up)
    gsend("y3", (-1, 0), GA_, over)
    gwait("ma", (1, 0), GA_)
    gsend("m5", (1, 0), GA1, down)
    gsend("y4", (1, 0), GA_, over)
    to_sib((-1, 0), GA_)
    to_sib((1, 0), GA_)
    gwait("y1", (0, 1), GB_)
    gsend("p7", (0, 1), GB0, up)
    gsend("m7", (0, 1), GB1, down)
    to_sib((0, 1), GB_)
    gwait("pb", (-1, 0), GB_)
    gsend("p6", (-1, 0), GB0, up)
    gsend("p8", (0, 1), GB1, up)
    gwait("mb", (1, 0), GB_)
    gsend("m6", (1, 0), GB1, down)
    gsend("m8", (0, 1), GB0, down)
    to_sib((1, 0), GB_)
    to_sib((-1, 0), GB_)
    gwait("y2", (0, 1), GA_)
    to_sib((0, 1), GA_)
    send_filter(3, 5, 1, 7)
    gwait("p5", (2, 0), GA0)
    gsend("y5", (2, 0), GA0, over)
    gwait("m5", (2, 0), GA1)
    gsend("y6", (2, 0), GA1, over)
    to_sib((2, 0), GA0, GA1)
    both((1, 0))
    both((-1, 0))
    gwait("p7", (-1, 1), GB0)
    gsend("p9", (-1, 1), GB0, up)
    gwait("m7", (1, 1), GB1)
    gsend("m9", (1, 1), GB1, down)
    to_sib((-1, 1), GB0)
    to_sib((1, 1), GB1)
    both((0, 1))
    gwait("y3", (-1, 1), GA_)
    to_sib((-1, 1), GA_)
    gwait("p6", (2, 0), GB0)
    gwait("m6", (2, 0), GB1)
    to_sib((2, 0), GB0, GB1)
    both((2, 0))
    gwait("y4", (1, 1), GA_)
    to_sib((1, 1), GA_)
    gwait("p8", (-1, 1), GB1)
    gwait("m8", (1, 1), GB0)
    to_sib((-1, 1), GB1)
    to_sib((1, 1), GB0)
    ready((-1, 1))
    project(acc_v, WV, (-1, 1))
    ready((1, 1))
    project(acc_v, WV, (1, 1))
    last = (2, 1)
    gwait("y5", last, GA0)
    to_sib(last, GA0)
    gwait("y6", last, GA1)
    to_sib(last, GA1)
    project(acc_g, WG, (-1, 1))
    gwait("p9", last, GB0)
    to_sib(last, GB0)
    gwait("m9", last, GB1)
    to_sib(last, GB1)
    w_in[last][0].wait()
    w_in[last][1].wait()
    project(acc_v, WV, last, cores=(c,))
    from_sib(last)
    project(acc_v, WV, last, cores=(other,))

    for p in range(4):
        cols = slice(128 * p, 128 * p + 128)
        pack_into(VS, p, acc_v[:HALF, cols], acc_v[HALF:, cols])
    for k in (4, 3, 5, 2, 6, 1, 7):
        send("v_%d" % k, VS.at[ring(k)], XR.at[ctx], (ring(k), ch))
    XR[ctx] = VS[ctx]
    project(acc_g, WG, (1, 1))
    project(acc_g, WG, last)

    fwd_in.wait()
    inv_in.wait()
    for k in range(1, CTX):
        arrived("h_%d" % k, HR.at[ring(CTX - k)])

    def spread_filter(i, carry):
        lo = low_lanes(HALF)
        h = HR[i].astype(F32)
        s = swap(h)
        HQ[pl.ds(pl.multiple_of(i * N, N), HALF), :] = jnp.where(lo, h, s).astype(BF16)
        HQ[pl.ds(pl.multiple_of(i * N + HALF, HALF), HALF), :] = jnp.where(lo, s, h).astype(BF16)
        return carry

    lax.fori_loop(0, CTX, spread_filter, 0)

    def filter_spectra(j, carry):
        b0 = HQ[pl.ds(pl.multiple_of(j * N, N), HALF), :]
        b1 = HQ[pl.ds(pl.multiple_of(j * N + HALF, HALF), HALF), :]
        s = dot(FWD[...], jnp.concatenate([b0, b1], axis=1))
        HS[2 * j] = s[:, :128]
        HS[2 * j + 1] = s[:, 128:]
        return carry

    lax.fori_loop(0, 8, filter_spectra, 0)

    def value_spectrum(i):
        XS[i] = dot(FWD[...], XR[i])

    value_spectrum(ctx)

    for k in (1, 7, 2, 6, 3, 5, 4):
        i = ring(CTX - k)
        arrived("v_%d" % k, XR.at[i])
        value_spectrum(i)

    lo = low_lanes(HALF)

    def multiply(even):
        def body(t, carry):
            re = pl.ds(pl.multiple_of(t * 8, 8), 8)
            im = pl.ds(pl.multiple_of(t * 8 + HALF, 8), 8)
            lo8 = low_lanes(8)
            xr, xi = [], []
            pr = pi = jnp.zeros((8, 128), F32)
            for i in range(8):
                ur, ui = XS[i, re, :], XS[i, im, :]
                mr = swap(jnp.where(lo8, ur, pr))
                mi = swap(jnp.where(lo8, ui, pi))
                if even:
                    xr += [pr + mi, mr + ui]
                    xi += [pi - mr, mi - ur]
                else:
                    xr += [pr - mi, mr - ui]
                    xi += [pi + mr, mi + ur]
                pr, pi = ur, ui
            yr, yi = [None] * 8, [None] * 8
            for d in range(16):
                hr, hi = HS[d, re, :], HS[d, im, :]
                for i in range(8):
                    s = 2 * i - d + 1
                    if s < 0:
                        continue
                    r = hr * xr[s] - hi * xi[s]
                    m = hr * xi[s] + hi * xr[s]
                    yr[i] = r if yr[i] is None else yr[i] + r
                    yi[i] = m if yi[i] is None else yi[i] + m
            for i in range(8):
                YP[i, re, :] = yr[i]
                YP[i, im, :] = yi[i]
            return carry

        return body

    lax.fori_loop(0, HALF // 16, multiply(True), 0)
    lax.fori_loop(HALF // 16, HALF // 8, multiply(False), 0)

    for w in range(2):
        for k in (4, 3, 5, 2, 6, 1, 7, 0):
            i = ring(k)
            y = dot(INV[pl.ds(QUARTER * w, QUARTER), :], YP[i].astype(BF16)).astype(BF16)
            if k:
                YS[w, i] = y
                send("y%d_%d" % (w, k), YS.at[w, i], YR.at[w, ctx], (i, ch))
            else:
                YR[w, ctx] = y

    def wave_rows(w):
        return pl.ds(HALF * w, HALF)

    def gate_wave(w):
        for k in range(1, CTX):
            arrived("y%d_%d" % (w, k), YR.at[w, ring(CTX - k)])
        lo = low_lanes(QUARTER)
        r = HALF * w
        for p in range(4):
            cols = slice(128 * p, 128 * p + 128)
            r0, r1 = YR[w, 2 * p].astype(F32), YR[w, 2 * p + 1].astype(F32)
            top = acc_g[QUARTER * w : QUARTER * w + QUARTER, cols].astype(BF16).astype(F32)
            bot = acc_g[HALF + QUARTER * w : HALF + QUARTER * w + QUARTER, cols].astype(BF16).astype(F32)
            GA[r : r + QUARTER, cols] = (jnp.where(lo, r0, swap(r1)) * top).astype(BF16)
            GA[r + QUARTER : r + HALF, cols] = (jnp.where(lo, swap(r0), r1) * bot).astype(BF16)
            send("a%d_%d" % (w, p), GA.at[wave_rows(w), cols], GB.at[wave_rows(w), cols], sib)

    def gate_arrived(w):
        for p in range(4):
            arrived("a%d_%d" % (w, p), GB.at[wave_rows(w), 128 * p : 128 * p + 128])

    gate_wave(0)
    drain("g_")
    for cp in wo_in:
        cp.wait()
    for q in range(CHIPS):
        arrived("w_%d" % q, WO.at[q, pl.ds(N, N)])
    gate_arrived(0)

    def mix(w, *ds):
        rows = wave_rows(w)
        for d in ds:
            q = chip(*d)

            def body(n, carry):
                cols = pl.ds(pl.multiple_of(n * 256, 256), 256)
                total = dot(GA[rows, :], WO[q, :N, cols]) + dot(GB[rows, :], WO[q, N:, cols])
                G[q, rows, cols] = total.astype(BF16)
                return carry

            lax.fori_loop(0, 2, body, 0)

    def cut(ref, start, size):
        return ref.at[pl.ds(start, size)]

    place, room = {}, [0, 0]
    for w in range(2):
        A0, A1, A, B0, B1, B = WAVES[w]
        for name, up_part, down_part in (
            ("z2y", B0, B1), ("z2o", B0, B1), ("z1y0", B0, B1), ("z1y1", B1, B0), ("z1o0", B0, B1),
            ("z1o1", B1, B0), ("a2", A0, A1), ("a1x", A1, A0), ("a1y", A0, A1),
        ):
            for side, part in ((0, up_part), (1, down_part)):
                place["pm"[side] + name, w] = (room[side], part[1])
                room[side] += part[1]

    def inbox(name, w):
        return cut(RP if name[0] == "p" else RM, *place[name, w])

    def ya(k, w):
        return RYA.at[w, k, pl.ds(0, WAVES[w][2][1])]

    def yb(w):
        return RYB.at[w, pl.ds(0, WAVES[w][5][1])]

    def sums(d, part):
        return G.at[chip(*d), rows_of(part)]

    def pass_on(name, w, d, part):
        send("r%d_%s" % (w, name), sums(d, part), inbox(name, w), up if name[0] == "p" else down)

    def add(name, w, d, part, buf=None):
        buf = inbox(name, w) if buf is None else buf
        arrived("r%d_%s" % (w, name), buf)
        ref = sums(d, part)
        ref[...] = (ref[...].astype(F32) + buf[...].astype(F32)).astype(BF16)

    def across(k, w, d):
        send("r%d_ya%d" % (w, k), sums(d, WAVES[w][2]), ya(k, w), over)

    def open_wave(w):
        A0, A1, A, B0, B1, B = WAVES[w]
        mix(w, (2, 1))
        across(0, w, (2, 1))
        pass_on("pz2y", w, (2, 1), B0)
        pass_on("mz2y", w, (2, 1), B1)
        mix(w, (2, 0))
        pass_on("pz2o", w, (2, 0), B0)
        pass_on("mz2o", w, (2, 0), B1)
        mix(w, (1, 1), (-1, 1))
        across(1, w, (1, 1))
        across(2, w, (-1, 1))
        pass_on("pz1y1", w, (1, 1), B1)
        pass_on("mz1y1", w, (-1, 1), B0)
        mix(w, (0, 1))
        across(3, w, (0, 1))
        mix(w, (1, 0), (-1, 0))
        pass_on("pz1o1", w, (1, 0), B1)
        pass_on("mz1o1", w, (-1, 0), B0)
        mix(w, (0, 0))

    def early(w):
        A0, A1, A, B0, B1, B = WAVES[w]
        add("pz2y", w, (1, 1), B0)
        pass_on("pz1y0", w, (1, 1), B0)
        add("mz2y", w, (-1, 1), B1)
        pass_on("mz1y0", w, (-1, 1), B1)
        add("ya0", w, (2, 0), A, ya(0, w))
        pass_on("pa2", w, (2, 0), A0)
        pass_on("ma2", w, (2, 0), A1)
        add("pz2o", w, (1, 0), B0)
        pass_on("pz1o0", w, (1, 0), B0)
        add("mz2o", w, (-1, 0), B1)
        pass_on("mz1o0", w, (-1, 0), B1)

    def middle(w):
        A0, A1, A, B0, B1, B = WAVES[w]
        add("pz1y1", w, (0, 1), B1)
        add("mz1y1", w, (0, 1), B0)
        add("ya1", w, (1, 0), A, ya(1, w))
        pass_on("pa1x", w, (1, 0), A1)
        add("ya2", w, (-1, 0), A, ya(2, w))
        pass_on("ma1x", w, (-1, 0), A0)
        add("pz1y0", w, (0, 1), B0)
        add("mz1y0", w, (0, 1), B1)
        send("r%d_yb" % w, sums((0, 1), B), yb(w), over)
        add("pa2", w, (1, 0), A0)
        pass_on("pa1y", w, (1, 0), A0)
        add("ma2", w, (-1, 0), A1)
        pass_on("ma1y", w, (-1, 0), A1)

    def total(w, part, *bufs):
        base, (start, size) = HALF * w, part
        border = base + QUARTER
        for lo_row, hi_row in ((start, min(start + size, border)), (max(start, border), start + size)):
            if lo_row >= hi_row:
                continue
            n = hi_row - lo_row
            value = sums((0, 0), (lo_row, n))[...].astype(F32)
            for b in bufs:
                value = value + cut(b, lo_row - start, n)[...].astype(F32)
            u = lo_row - base
            real = QUARTER * w + (u if u < QUARTER else u - QUARTER + HALF)
            out_ref[pl.ds(real, n), :] = value.astype(BF16)

    def close_wave(w):
        A0, A1, A, B0, B1, B = WAVES[w]
        arrived("r%d_ya3" % w, ya(3, w))
        for name in ("pz1o1", "mz1o1", "pz1o0", "mz1o0"):
            arrived("r%d_%s" % (w, name), inbox(name, w))
        for name in ("pa1x", "ma1x", "pa1y", "ma1y"):
            arrived("r%d_%s" % (w, name), inbox(name, w))
        total(w, A0, cut(ya(3, w), 0, A0[1]), inbox("pa1y", w), inbox("ma1x", w))
        total(w, A1, cut(ya(3, w), A0[1], A1[1]), inbox("pa1x", w), inbox("ma1y", w))
        arrived("r%d_yb" % w, yb(w))
        total(w, B0, inbox("pz1o0", w), inbox("mz1o1", w), cut(yb(w), 0, B0[1]))
        total(w, B1, inbox("pz1o1", w), inbox("mz1o0", w), cut(yb(w), B0[1], B1[1]))

    open_wave(0)
    gate_wave(1)
    gate_arrived(1)
    open_wave(1)
    early(0)
    middle(0)
    early(1)
    close_wave(0)
    middle(1)
    close_wave(1)
    drain("")


def on_device(tokens, proj_value, proj_gate, conv_filter, proj_output):
    forward, inverse = tables()
    anywhere = pl.BlockSpec(memory_space=pl.ANY)
    vm = pltpu.VMEM
    return pl.pallas_call(
        kernel,
        out_shape=pltpu.VMEM((N, N), BF16),
        in_specs=[anywhere] * 7,
        out_specs=pl.BlockSpec(memory_space=pltpu.VMEM),
        scratch_shapes=[
            vm((16, N, N), BF16),
            vm((8192, N), BF16),
            vm((8192, N), BF16),
            vm((CHIPS, 2 * N, N), BF16),
            vm((2 * HALF, HALF), BF16),
            vm((HALF, 2 * HALF), BF16),
            vm((N, N), BF16),
            vm((N, N), F32),
            vm((N, N), F32),
            vm((CTX, HALF, 128), BF16),
            vm((CTX, HALF, 128), BF16),
            vm((CTX, HALF, 128), BF16),
            vm((CTX, HALF, 128), BF16),
            vm((2, CTX, QUARTER, 128), BF16),
            vm((2, CTX, QUARTER, 128), BF16),
            vm((16 * HALF, 128), BF16),
            vm((8, N, 128), F32),
            vm((16, N, 128), F32),
            vm((8, N, 128), F32),
            vm((N, N), BF16),
            vm((N, N), BF16),
            vm((2, 4, 112, N), BF16),
            vm((2, 160, N), BF16),
            vm((1232, N), BF16),
            vm((1216, N), BF16),
            pltpu.SemaphoreType.DMA((TRANSFERS,)),
            pltpu.SemaphoreType.DMA((TRANSFERS,)),
            pltpu.SemaphoreType.DMA((40,)),
        ],
        compiler_params=pltpu.CompilerParams(
            collective_id=0, has_side_effects=True, vmem_limit_bytes=56 * 2**20
        ),
        name="hyena_block",
    )(
        tokens, proj_value, proj_gate, conv_filter, proj_output,
        jnp.asarray(forward), jnp.asarray(inverse),
    )


def solution(mesh):
    in_specs = (P("ctx", "ch"), P(None, "ch"), P(None, "ch"), P("ch", "ctx"), P("ch", None))
    return jax.shard_map(
        on_device, mesh=mesh, in_specs=in_specs, out_specs=P("ctx", "ch"), check_vma=False
    )
```
